32 devices in a mesh: frag: 4 (over y, x), orb: 8 (over z, core).
Axes of the slice: x: 2, y: 2, z: 4, core: 2. Of those that a mesh axis runs over, the one named last changes fastest.
Arguments:
- orbitals: float32 [8, 128, 48, 2304], P('frag', 'orb'), may hold values from -6 to 6
- potential: float32 [24, 36864], P('frag', 'orb'), may hold values from -3 to 0
- ion_potential: float32 [24, 36864], P('frag', 'orb'), may hold values from -2 to 0
- core_density: float32 [24, 36864], P('frag', 'orb'), may hold values from 0.5 to 2
- frag_blocks: int32 [8, 3], replicated, may hold values from 0 to 23, as said below
- frag_signs: int32 [8], replicated, may hold values from -1 to 1, as said below
Outputs:
- filtered: float32 [8, 128, 48, 2304], P('frag', 'orb')
- new_potential: float32 [24, 36864], P('frag', 'orb')
The draws below stay inside these ranges and needn't reach their ends.
Inputs may be any that keep to these rules, and one draw needn't show every extreme that they name: `frag_blocks`: fragments g * 2 to (g + 1) * 2 - 1 form group g; block b belongs to owner b // 6. Among the 6 entries of one group no owner is named more than 3 times, and group g names owner (g + s) mod 4 exactly 3 times, for a shift s common to all groups. The first and the last block of every owner are named. `frag_signs`: each sign is +1 or -1.
All inputs are finite; a program needn't handle non-finite values.
Results may differ from the reference program's by a relative error of at most 0.0001.
Values sent between devices are 32-bit elements; how exact they have to be, the bound alone decides.
A program may use at most 192 MiB of HBM per device.

```python
import math
import jax
import jax.numpy as jnp
from jax import lax

G = 48
FB = 3
ORBS = 128
ITERS = 2
FRAG_DEV = 2
FRAGS = 8
BLOCK = 36864
BLK_DEV = 6
NBLK = 24
CAP = 3
N_FRAG = 4


def draw_frag_blocks(key, part):
    entries = FRAG_DEV * FB
    others = entries - CAP
    subkeys = jax.random.split(jax.random.fold_in(key, 11), 4)
    shift_value = jax.random.randint(subkeys[0], (), 0, N_FRAG)
    busiest = (jnp.arange(N_FRAG, dtype=jnp.int32) + shift_value) % N_FRAG
    offsets = jax.random.randint(subkeys[1], (N_FRAG, others), 1, N_FRAG)
    owners = jnp.concatenate([jnp.broadcast_to(busiest[:, None], (N_FRAG, CAP)), (busiest[:, None] + offsets) % N_FRAG], axis=1)
    local_ids = jax.random.randint(subkeys[2], (N_FRAG, entries), 0, BLK_DEV)
    local_ids = local_ids.at[:, 0].set(BLK_DEV - 1)
    local_ids = local_ids.at[:, 1].set(0)
    scores = jax.random.randint(subkeys[3], (N_FRAG, entries), 0, 1048576) * entries + jnp.arange(entries, dtype=jnp.int32)[None, :]
    ordering = jnp.argsort(scores, axis=1)
    owners = jnp.take_along_axis(owners, ordering, axis=1)
    local_ids = jnp.take_along_axis(local_ids, ordering, axis=1)
    blocks = owners * BLK_DEV + local_ids
    return blocks.reshape(FRAGS, FB).astype(jnp.int32)


def draw_frag_signs(key, part):
    coins = jax.random.randint(jax.random.fold_in(key, 23), (FRAGS,), 0, 2)
    return (2 * coins - 1).astype(jnp.int32)


def levels(stream_key, dims, cuts, low, high):
    factor_of = 1.0
    for dim, parts in cuts:
        draws = jax.random.uniform(jax.random.fold_in(jax.random.fold_in(stream_key, 6), dim), (parts,), jnp.float32, low / len(cuts), high / len(cuts))
        factor_of = factor_of * jnp.repeat(jnp.exp(draws), dims[dim] // parts).reshape((-1,) + (1,) * (len(dims) - 1 - dim))
    return factor_of


def normal_values(key, shape, scale, most, cuts=(), kind=jnp.bfloat16):
    loudness = levels(key, shape, cuts, -0.22, 0.18) if cuts else 1.0
    values = jax.random.normal(key, shape, jnp.float32) * scale * loudness
    return jnp.minimum(jnp.maximum(values, -most), most).astype(kind)


def setup_inputs(seed: int = 0) -> dict:
    key_list = jax.random.split(jax.random.key(seed), 7)
    return {
        "orbitals": normal_values(key_list[0], (FRAGS, ORBS, G, G * G), 1.0, 6.0, ((0, 4), (1, 8)), jnp.float32),
        "potential": jnp.clip(-3.0 + 3.0 * jax.random.uniform(key_list[1], (NBLK, BLOCK), jnp.float32) ** levels(key_list[1], (NBLK, BLOCK), ((0, 4), (1, 8)), -0.2, 0.2), -3.0, 0.0),
        "ion_potential": jnp.clip(-2.0 + 2.0 * jax.random.uniform(key_list[2], (NBLK, BLOCK), jnp.float32) ** levels(key_list[2], (NBLK, BLOCK), ((0, 4), (1, 8)), -0.2, 0.2), -2.0, 0.0),
        "core_density": jnp.clip(jnp.exp(math.log(2.0) - 1.3862944 * jax.random.uniform(key_list[3], (NBLK, BLOCK), jnp.float32) ** levels(key_list[3], (NBLK, BLOCK), ((0, 4), (1, 8)), -0.2, 0.2)), 0.5, 2.0),
        "frag_blocks": draw_frag_blocks(jax.random.fold_in(key_list[6], 71), 0),
        "frag_signs": draw_frag_signs(jax.random.fold_in(key_list[6], 71), 0),
    }


SPACING = 0.5
FILTER_CENTER = 18.0
FILTER_HALF = 16.0
DENSITY_FLOOR = 0.25
EXCHANGE_COEF = 0.9847450218426965
NORM_EPS = 1e-06

def laplacian(values):
    side_cells = values.shape[-2]
    plane_cells = values.shape[-1]
    leading = [(0, 0)] * (values.ndim - 2)
    padded_x = jnp.pad(values, leading + [(2, 2), (0, 0)])
    nearest = padded_x[..., 1:side_cells + 1, :] + padded_x[..., 3:side_cells + 3, :]
    distant = padded_x[..., 0:side_cells, :] + padded_x[..., 4:side_cells + 4, :]
    padded_y = jnp.pad(values, leading + [(0, 0), (2 * side_cells, 2 * side_cells)])
    nearest = nearest + padded_y[..., side_cells:side_cells + plane_cells] + padded_y[..., 3 * side_cells:3 * side_cells + plane_cells]
    distant = distant + padded_y[..., 0:plane_cells] + padded_y[..., 4 * side_cells:4 * side_cells + plane_cells]
    padded_z = jnp.pad(values, leading + [(0, 0), (2, 2)])
    column = jnp.arange(plane_cells, dtype=jnp.int32) % side_cells
    nearest = nearest + jnp.where(column >= 1, padded_z[..., 1:1 + plane_cells], 0.0)
    nearest = nearest + jnp.where(column <= side_cells - 2, padded_z[..., 3:3 + plane_cells], 0.0)
    distant = distant + jnp.where(column >= 2, padded_z[..., 0:plane_cells], 0.0)
    distant = distant + jnp.where(column <= side_cells - 3, padded_z[..., 4:4 + plane_cells], 0.0)
    return (16.0 * nearest - distant - 90.0 * values) / 12.0

def hamiltonian(values, local_pot):
    return -0.5 / (SPACING * SPACING) * laplacian(values) + local_pot * values

def chebyshev(values, local_pot):
    previous = values
    current = (hamiltonian(values, local_pot) - FILTER_CENTER * values) / FILTER_HALF
    for degree in range(3):
        further = 2.0 * (hamiltonian(current, local_pot) - FILTER_CENTER * current) / FILTER_HALF - previous
        previous, current = (current, further)
    magnitude = jnp.sqrt(lax.optimization_barrier(jnp.mean(current * current, axis=(-2, -1), keepdims=True)) + NORM_EPS)
    return current / magnitude

def filter_fragment(operands):
    orbital_block, local_pot = operands
    result = chebyshev(orbital_block, local_pot)
    density = lax.optimization_barrier(jnp.sum(result * result, axis=0)) / ORBS
    return (result, density)

def reference(orbitals, potential, ion_potential, core_density, frag_blocks, frag_signs):
    entries = frag_blocks.reshape(-1).astype(jnp.int32)
    entry_signs = jnp.repeat(frag_signs, FB).astype(jnp.float32)
    current_pot = potential
    orbital_set = orbitals
    for iteration in range(ITERS):
        frag_pot = jnp.take(current_pot, entries, axis=0).reshape(FRAGS, 1, G, G * G)
        orbital_set, density = lax.map(filter_fragment, (orbital_set, frag_pot))
        pieces = density.reshape(FRAGS * FB, BLOCK) * entry_signs[:, None]
        total = core_density.at[entries].add(pieces)
        current_pot = ion_potential - EXCHANGE_COEF * jnp.cbrt(jnp.maximum(total, DENSITY_FLOOR))
    return (orbital_set, current_pot)
```

```python
import functools

import jax
import jax.numpy as jnp
import numpy as np
from jax import lax
from jax.experimental import pallas as pl
from jax.experimental.pallas import tpu as pltpu
from jax.sharding import PartitionSpec as P

FB = 3
ORBS = 128
ITERS = 2
CAP = 3

DENSITY_FLOOR = 0.25
EXCHANGE_COEF = 0.9847450218426965
NORM_EPS = 1e-06

LANE = 128
NB = 256


def band_weights(side):
    period = side // np.gcd(NB, side)
    mats = []
    for phase in range(int(period)):
        out = NB * phase + np.arange(NB)[None, :]
        inp = NB * phase - LANE + np.arange(NB + 2 * LANE)[:, None]
        diff = inp - out
        same = (inp // side) == (out // side)
        near = (same & (np.abs(diff) == 1)) | (np.abs(diff) == side)
        far = (same & (np.abs(diff) == 2)) | (np.abs(diff) == 2 * side)
        mat = np.where(near, -16.0, 0.0) + np.where(far, 1.0, 0.0)
        mat = mat.reshape(-1, 1, LANE, NB)
        mats.append(np.concatenate([mat, mat], axis=1).reshape(-1, NB))
    return jnp.asarray(np.stack(mats), dtype=jnp.bfloat16)


def filter_kernel(first, frag, orbs, side, plane, *refs):
    orb_ref, pot_ref, band_ref = refs[:3]
    out_ref, dens_ref, ybuf, zbuf, hly, hlz, wbuf, sems = refs[-8:]
    blocks = plane // NB
    tiles = plane // LANE
    period = band_ref.shape[0]
    xc = 16 // orbs
    rows_chunk = orbs * side // 3
    x_chunk = rows_chunk // 16
    inv48 = 1.0 / 48.0

    if first:
        copies = [
            pltpu.make_async_copy(
                orb_ref.at[frag, o], ybuf.at[pl.ds(2, side), o, :], sems.at[o]
            )
            for o in range(orbs)
        ]
    else:
        copies = [pltpu.make_async_copy(orb_ref, ybuf.at[pl.ds(2, side)], sems.at[0])]
    for copy in copies:
        copy.start()
    wbuf[...] = (pot_ref[...] - 3.0) * 0.125
    for buf in (ybuf, zbuf):
        buf[pl.ds(0, 2)] = jnp.zeros((2, orbs, plane), jnp.float32)
        buf[pl.ds(side + 2, 2)] = jnp.zeros((2, orbs, plane), jnp.float32)
    rows = hly.shape[0]
    for buf in (hly, hlz):
        buf[:, pl.ds(0, NB)] = jnp.zeros((rows, NB), jnp.bfloat16)
        buf[:, pl.ds(NB * (tiles + 1), NB)] = jnp.zeros((rows, NB), jnp.bfloat16)
    for copy in copies:
        copy.wait()

    def split(dst, row, lane, new):
        high = new.astype(jnp.bfloat16)
        low = (new - high.astype(jnp.float32)).astype(jnp.bfloat16)
        for half in range(NB // LANE):
            part = slice(half * LANE, (half + 1) * LANE)
            at = pl.multiple_of(2 * lane + NB * (half + 1), NB)
            dst[pl.ds(row, 16), pl.ds(at, LANE)] = high[:, part]
            dst[pl.ds(row, 16), pl.ds(at + LANE, LANE)] = low[:, part]

    def split_block(i, carry):
        x = i * xc
        for b in range(blocks):
            value = ybuf[pl.ds(x + 2, xc), :, pl.ds(b * NB, NB)].reshape(16, NB)
            split(hly, pl.multiple_of(i * 16, 16), b * NB, value)
        return carry

    lax.fori_loop(0, side // xc, split_block, 0)

    def step(cur, dst, hl_cur, hl_next, start, last):
        def block(b, carry):
            lane = pl.multiple_of(b * NB, NB)
            weights = band_ref[lax.rem(b, period)]

            def product(c):
                return jnp.dot(
                    hl_cur[pl.ds(c * rows_chunk, rows_chunk), pl.ds(2 * lane, 4 * NB)],
                    weights,
                    preferred_element_type=jnp.float32,
                )

            def update(c, prod, acc):
                for j in range(x_chunk):
                    i = c * x_chunk + j
                    x = i * xc

                    def plane_at(buf, offset):
                        return buf[pl.ds(x + 2 + offset, xc), :, pl.ds(lane, NB)].reshape(16, NB)

                    near = plane_at(cur, -1) + plane_at(cur, 1)
                    far = plane_at(cur, -2) + plane_at(cur, 2)
                    total = prod[j * 16 : (j + 1) * 16] + (far - 16.0 * near)
                    w = wbuf[pl.ds(x, xc), pl.ds(lane, NB)]
                    w = jnp.broadcast_to(w[:, None, :], (xc, orbs, NB)).reshape(16, NB)
                    new = total * inv48 + w * plane_at(cur, 0)
                    if start:
                        new = new * 0.5
                    else:
                        new = new - plane_at(dst, 0)
                    dst[pl.ds(x + 2, xc), :, pl.ds(lane, NB)] = new.reshape(xc, orbs, NB)
                    if last:
                        acc = acc + new * new
                    else:
                        split(hl_next, i * 16, lane, new)
                return acc

            acc = carry
            count = rows // rows_chunk
            prods = [product(0)]
            for c in range(count):
                if c + 1 < count:
                    prods.append(product(c + 1))
                acc = update(c, prods[c], acc)
            return acc

        return lax.fori_loop(0, blocks, block, jnp.zeros((16, NB), jnp.float32))

    step(ybuf, zbuf, hly, hlz, True, False)
    step(zbuf, ybuf, hlz, hly, False, False)
    step(ybuf, zbuf, hly, hlz, False, False)
    acc = step(zbuf, ybuf, hlz, hly, False, True)
    square = jnp.sum(acc, axis=1, keepdims=True).reshape(xc, orbs, 1)
    square = jnp.sum(square, axis=0)
    scale = 1.0 / jnp.sqrt(square * (1.0 / (side * plane)) + NORM_EPS)
    scale = jnp.broadcast_to(scale, (orbs, NB))

    def finish(i, carry):
        x = pl.multiple_of(i * 8, 8)
        for b in range(blocks):
            lanes = pl.ds(b * NB, NB)
            value = ybuf[pl.ds(x + 2, 8), :, lanes] * scale[None]
            ybuf[pl.ds(x + 2, 8), :, lanes] = value
            dens_ref[pl.ds(x, 8), lanes] = jnp.sum(value * value, axis=1)
        return carry

    lax.fori_loop(0, side // 8, finish, 0)
    if first:
        outs = [pltpu.make_async_copy(ybuf.at[pl.ds(2, side)], out_ref, sems.at[0])]
    else:
        outs = [
            pltpu.make_async_copy(
                ybuf.at[pl.ds(2, side), o, :], out_ref.at[frag, o], sems.at[o]
            )
            for o in range(orbs)
        ]
    for copy in outs:
        copy.start()
    for copy in outs:
        copy.wait()


def filter_call(first, frag, shape, source, pot, band, previous):
    count, orbs, side, plane = shape
    rows = orbs * side
    body = functools.partial(filter_kernel, first, frag, orbs, side, plane)
    vmem = pl.BlockSpec(memory_space=pltpu.VMEM)
    hbm = pl.BlockSpec(memory_space=pl.ANY)
    in_specs = [hbm, vmem, vmem]
    operands = [source, pot, band]
    aliases = {}
    if first:
        out = jax.ShapeDtypeStruct((side, orbs, plane), jnp.float32)
    else:
        out = jax.ShapeDtypeStruct(shape, jnp.float32)
        if previous is not None:
            in_specs.append(hbm)
            operands.append(previous)
            aliases = {3: 0}
    wide = 2 * plane + 2 * NB
    return pl.pallas_call(
        body,
        out_shape=(out, jax.ShapeDtypeStruct((side, plane), jnp.float32)),
        in_specs=in_specs,
        out_specs=(hbm, vmem),
        input_output_aliases=aliases,
        scratch_shapes=[
            pltpu.VMEM((side + 4, orbs, plane), jnp.float32),
            pltpu.VMEM((side + 4, orbs, plane), jnp.float32),
            pltpu.VMEM((rows, wide), jnp.bfloat16),
            pltpu.VMEM((rows, wide), jnp.bfloat16),
            pltpu.VMEM((side, plane), jnp.float32),
            pltpu.SemaphoreType.DMA((orbs,)),
        ],
        compiler_params=pltpu.CompilerParams(vmem_limit_bytes=48 * 1024 * 1024),
        cost_estimate=pl.CostEstimate(
            flops=4 * 2 * rows * plane * 1024,
            bytes_accessed=8 * rows * plane,
            transcendentals=0,
        ),
        name="filter_fragment",
    )(*operands)


def owner_tables(frag_blocks, block_count, groups):
    entries = frag_blocks.reshape(groups, -1)
    owners = entries // block_count
    count = entries.shape[1]
    positions = jnp.arange(count, dtype=jnp.int32)
    earlier = positions[:, None] > positions[None, :]
    same_owner = owners[:, :, None] == owners[:, None, :]
    ranks = jnp.sum(jnp.where(same_owner & earlier[None, :, :], 1, 0), axis=2).astype(jnp.int32)
    return (entries, owners, ranks)


def shards(orbitals, potential, ion_potential, core_density, frag_blocks, frag_signs):
    groups = lax.axis_size("frag")
    me_index = lax.axis_index("frag")
    side = orbitals.shape[2]
    plane = orbitals.shape[3]
    frag_count = orbitals.shape[0]
    block_count = potential.shape[0]
    piece_cells = potential.shape[1]
    capacity = CAP
    band = band_weights(side)
    entries, owners, ranks = owner_tables(frag_blocks, block_count, groups)
    count = entries.shape[1]
    slot_range = jnp.arange(capacity, dtype=jnp.int32)
    send_match = (owners[:, None, :] == me_index) & (ranks[:, None, :] == slot_range[None, :, None])
    send_valid = jnp.any(send_match, axis=2).reshape(-1)
    send_block = jnp.sum(
        jnp.where(send_match, entries[:, None, :] - me_index * block_count, 0), axis=2
    ).reshape(-1)
    send_mask = send_valid.astype(jnp.float32)[:, None]
    my_owners = lax.dynamic_index_in_dim(owners, me_index, 0, keepdims=False)
    my_ranks = lax.dynamic_index_in_dim(ranks, me_index, 0, keepdims=False)
    my_slot = my_owners * capacity + my_ranks
    owner_range = jnp.arange(groups, dtype=jnp.int32)
    back_match = (my_owners[None, None, :] == owner_range[:, None, None]) & (
        my_ranks[None, None, :] == slot_range[None, :, None]
    )
    back_mask = jnp.any(back_match, axis=2).reshape(-1).astype(jnp.float32)[:, None]
    entry_range = jnp.arange(count, dtype=jnp.int32)
    back_entry = jnp.sum(jnp.where(back_match, entry_range[None, None, :], 0), axis=2).reshape(-1)
    my_signs = jnp.repeat(
        lax.dynamic_slice_in_dim(frag_signs, me_index * frag_count, frag_count), FB
    ).astype(jnp.float32)
    block_range = jnp.arange(block_count, dtype=jnp.int32)
    selector = ((send_block[None, :] == block_range[:, None]) & send_valid[None, :]).astype(
        jnp.float32
    )
    current_pot = potential
    middle = None
    filtered = None
    for iteration in range(ITERS):
        outgoing = (jnp.take(current_pot, send_block, axis=0) * send_mask).reshape(
            groups, capacity, piece_cells
        )
        incoming = lax.all_to_all(outgoing, "frag", split_axis=0, concat_axis=0, tiled=True)
        sectioned = jnp.take(
            incoming.reshape(groups * capacity, piece_cells), my_slot, axis=0
        ).reshape(frag_count, FB, piece_cells)
        pieces = []
        next_middle = []
        for frag in range(frag_count):
            pot = lax.all_gather(sectioned[frag], "orb", axis=1, tiled=True).reshape(side, plane)
            if iteration == 0:
                result, dens = filter_call(True, frag, orbitals.shape, orbitals, pot, band, None)
                next_middle.append(result)
            else:
                filtered, dens = filter_call(
                    False, frag, orbitals.shape, middle[frag], pot, band, filtered
                )
            pieces.append(
                lax.psum_scatter(dens.reshape(FB, -1), "orb", scatter_dimension=1, tiled=True)
            )
        middle = next_middle
        summed = jnp.stack(pieces)
        signed = (summed / ORBS).reshape(count, piece_cells) * my_signs[:, None]
        returning = (jnp.take(signed, back_entry, axis=0) * back_mask).reshape(
            groups, capacity, piece_cells
        )
        arrived = lax.all_to_all(returning, "frag", split_axis=0, concat_axis=0, tiled=True)
        collected = jnp.dot(
            selector,
            arrived.reshape(groups * capacity, piece_cells),
            precision=lax.Precision.HIGHEST,
            preferred_element_type=jnp.float32,
        )
        total = core_density + collected
        current_pot = ion_potential - EXCHANGE_COEF * jnp.cbrt(jnp.maximum(total, DENSITY_FLOOR))
    return (filtered, current_pot)


def solution(mesh):
    in_specs = (
        P("frag", "orb", None, None),
        P("frag", "orb"),
        P("frag", "orb"),
        P("frag", "orb"),
        P(),
        P(),
    )
    out_specs = (P("frag", "orb", None, None), P("frag", "orb"))
    return jax.shard_map(shards, mesh=mesh, in_specs=in_specs, out_specs=out_specs, check_vma=False)
```

```python
import functools

import jax
import jax.numpy as jnp
import numpy as np
from jax import lax
from jax.experimental import pallas as pl
from jax.experimental.pallas import tpu as pltpu
from jax.sharding import PartitionSpec as P

FB = 3
ORBS = 128
ITERS = 2
CAP = 3

DENSITY_FLOOR = 0.25
EXCHANGE_COEF = 0.9847450218426965
NORM_EPS = 1e-06

LANE = 128
NB = 256


def band_weights(side):
    period = side // np.gcd(NB, side)
    mats = []
    for phase in range(int(period)):
        out = NB * phase + np.arange(NB)[None, :]
        inp = NB * phase - LANE + np.arange(NB + 2 * LANE)[:, None]
        diff = inp - out
        same = (inp // side) == (out // side)
        near = (same & (np.abs(diff) == 1)) | (np.abs(diff) == side)
        far = (same & (np.abs(diff) == 2)) | (np.abs(diff) == 2 * side)
        mat = np.where(near, -16.0, 0.0) + np.where(far, 1.0, 0.0)
        mat = mat.reshape(-1, 1, LANE, NB)
        mats.append(np.concatenate([mat, mat], axis=1).reshape(-1, NB))
    return jnp.asarray(np.stack(mats), dtype=jnp.bfloat16)


def filter_kernel(first, frag, orbs, side, plane, *refs):
    orb_ref, pot_ref, band_ref = refs[:3]
    out_ref, dens_ref, ybuf, zbuf, hly, hlz, wbuf, sems = refs[-8:]
    blocks = plane // NB
    tiles = plane // LANE
    period = band_ref.shape[0]
    xc = 16 // orbs
    rows_chunk = orbs * side // 3
    x_chunk = rows_chunk // 16
    inv48 = 1.0 / 48.0

    if first:
        copies = [
            pltpu.make_async_copy(
                orb_ref.at[frag, o], ybuf.at[pl.ds(2, side), o, :], sems.at[o]
            )
            for o in range(orbs)
        ]
    else:
        copies = [pltpu.make_async_copy(orb_ref, ybuf.at[pl.ds(2, side)], sems.at[0])]
    for copy in copies:
        copy.start()
    pieces, _, piece_rows, _ = pot_ref.shape
    piece_x = piece_rows // FB
    for d in range(pieces):
        for slot in range(FB):
            x = slot * (side // FB) + d * piece_x
            value = pot_ref[d, frag, slot * piece_x : (slot + 1) * piece_x]
            wbuf[x : x + piece_x] = (value - 3.0) * 0.125
    for buf in (ybuf, zbuf):
        buf[pl.ds(0, 2)] = jnp.zeros((2, orbs, plane), jnp.float32)
        buf[pl.ds(side + 2, 2)] = jnp.zeros((2, orbs, plane), jnp.float32)
    rows = hly.shape[0]
    for buf in (hly, hlz):
        buf[:, pl.ds(0, NB)] = jnp.zeros((rows, NB), jnp.bfloat16)
        buf[:, pl.ds(NB * (tiles + 1), NB)] = jnp.zeros((rows, NB), jnp.bfloat16)
    for copy in copies:
        copy.wait()

    def split(dst, row, lane, new):
        high = new.astype(jnp.bfloat16)
        low = (new - high.astype(jnp.float32)).astype(jnp.bfloat16)
        for half in range(NB // LANE):
            part = slice(half * LANE, (half + 1) * LANE)
            at = pl.multiple_of(2 * lane + NB * (half + 1), NB)
            dst[pl.ds(row, 16), pl.ds(at, LANE)] = high[:, part]
            dst[pl.ds(row, 16), pl.ds(at + LANE, LANE)] = low[:, part]

    def split_block(i, carry):
        x = i * xc
        for b in range(blocks):
            value = ybuf[pl.ds(x + 2, xc), :, pl.ds(b * NB, NB)].reshape(16, NB)
            split(hly, pl.multiple_of(i * 16, 16), b * NB, value)
        return carry

    lax.fori_loop(0, side // xc, split_block, 0)

    def step(cur, dst, hl_cur, hl_next, start, last):
        def block(b, carry):
            lane = pl.multiple_of(b * NB, NB)
            weights = band_ref[lax.rem(b, period)]

            def product(c):
                return jnp.dot(
                    hl_cur[pl.ds(c * rows_chunk, rows_chunk), pl.ds(2 * lane, 4 * NB)],
                    weights,
                    preferred_element_type=jnp.float32,
                )

            def update(c, prod, acc):
                for j in range(x_chunk):
                    i = c * x_chunk + j
                    x = i * xc

                    def plane_at(buf, offset):
                        return buf[pl.ds(x + 2 + offset, xc), :, pl.ds(lane, NB)].reshape(16, NB)

                    near = plane_at(cur, -1) + plane_at(cur, 1)
                    far = plane_at(cur, -2) + plane_at(cur, 2)
                    total = prod[j * 16 : (j + 1) * 16] + (far - 16.0 * near)
                    w = wbuf[pl.ds(x, xc), pl.ds(lane, NB)]
                    w = jnp.broadcast_to(w[:, None, :], (xc, orbs, NB)).reshape(16, NB)
                    new = total * inv48 + w * plane_at(cur, 0)
                    if start:
                        new = new * 0.5
                    else:
                        new = new - plane_at(dst, 0)
                    dst[pl.ds(x + 2, xc), :, pl.ds(lane, NB)] = new.reshape(xc, orbs, NB)
                    if last:
                        acc = acc + new * new
                    else:
                        split(hl_next, i * 16, lane, new)
                return acc

            acc = carry
            count = rows // rows_chunk
            prods = [product(0)]
            for c in range(count):
                if c + 1 < count:
                    prods.append(product(c + 1))
                acc = update(c, prods[c], acc)
            return acc

        return lax.fori_loop(0, blocks, block, jnp.zeros((16, NB), jnp.float32))

    step(ybuf, zbuf, hly, hlz, True, False)
    step(zbuf, ybuf, hlz, hly, False, False)
    step(ybuf, zbuf, hly, hlz, False, False)
    acc = step(zbuf, ybuf, hlz, hly, False, True)
    square = jnp.sum(acc, axis=1, keepdims=True).reshape(xc, orbs, 1)
    square = jnp.sum(square, axis=0)
    scale = 1.0 / jnp.sqrt(square * (1.0 / (side * plane)) + NORM_EPS)
    scale = jnp.broadcast_to(scale, (orbs, NB))

    def finish(d, carry):
        starts = [slot * (side // FB) + d * piece_x + 2 for slot in range(FB)]
        for b in range(blocks):
            lanes = pl.ds(b * NB, NB)
            sums = []
            for start in starts:
                value = ybuf[pl.ds(start, piece_x), :, lanes] * scale[None]
                ybuf[pl.ds(start, piece_x), :, lanes] = value
                sums.append(value * value)
            dens_ref[d, :, lanes] = jnp.sum(jnp.concatenate(sums, axis=0), axis=1)
        if first:
            for start in starts:
                slab(start).start()
        return carry

    def slab(start):
        rows_in = pl.ds(start, piece_x)
        rows_out = pl.ds(start - 2, piece_x)
        return pltpu.make_async_copy(ybuf.at[rows_in], out_ref.at[rows_out], sems.at[0])

    lax.fori_loop(0, pieces, finish, 0)
    if first:
        pltpu.make_async_copy(ybuf.at[pl.ds(2, side)], out_ref, sems.at[0]).wait()
    else:
        outs = [
            pltpu.make_async_copy(
                ybuf.at[pl.ds(2, side), o, :], out_ref.at[frag, o], sems.at[o]
            )
            for o in range(orbs)
        ]
        for copy in outs:
            copy.start()
        for copy in outs:
            copy.wait()


def filter_call(first, frag, shape, source, pot, band, previous):
    count, orbs, side, plane = shape
    rows = orbs * side
    body = functools.partial(filter_kernel, first, frag, orbs, side, plane)
    vmem = pl.BlockSpec(memory_space=pltpu.VMEM)
    hbm = pl.BlockSpec(memory_space=pl.ANY)
    in_specs = [hbm, vmem, vmem]
    operands = [source, pot, band]
    aliases = {}
    if first:
        out = jax.ShapeDtypeStruct((side, orbs, plane), jnp.float32)
    else:
        out = jax.ShapeDtypeStruct(shape, jnp.float32)
        if previous is not None:
            in_specs.append(hbm)
            operands.append(previous)
            aliases = {3: 0}
    wide = 2 * plane + 2 * NB
    dens = jax.ShapeDtypeStruct((pot.shape[0], pot.shape[2], plane), jnp.float32)
    return pl.pallas_call(
        body,
        out_shape=(out, dens),
        in_specs=in_specs,
        out_specs=(hbm, vmem),
        input_output_aliases=aliases,
        scratch_shapes=[
            pltpu.VMEM((side + 4, orbs, plane), jnp.float32),
            pltpu.VMEM((side + 4, orbs, plane), jnp.float32),
            pltpu.VMEM((rows, wide), jnp.bfloat16),
            pltpu.VMEM((rows, wide), jnp.bfloat16),
            pltpu.VMEM((side, plane), jnp.float32),
            pltpu.SemaphoreType.DMA((orbs,)),
        ],
        compiler_params=pltpu.CompilerParams(vmem_limit_bytes=48 * 1024 * 1024),
        cost_estimate=pl.CostEstimate(
            flops=4 * 2 * rows * plane * 1024,
            bytes_accessed=8 * rows * plane,
            transcendentals=0,
        ),
        name="filter_fragment",
    )(*operands)


def owner_tables(frag_blocks, block_count, groups):
    entries = frag_blocks.reshape(groups, -1)
    owners = entries // block_count
    count = entries.shape[1]
    positions = jnp.arange(count, dtype=jnp.int32)
    earlier = positions[:, None] > positions[None, :]
    same_owner = owners[:, :, None] == owners[:, None, :]
    ranks = jnp.sum(jnp.where(same_owner & earlier[None, :, :], 1, 0), axis=2).astype(jnp.int32)
    return (entries, owners, ranks)


def shards(orbitals, potential, ion_potential, core_density, frag_blocks, frag_signs):
    groups = lax.axis_size("frag")
    me_index = lax.axis_index("frag")
    side = orbitals.shape[2]
    plane = orbitals.shape[3]
    frag_count = orbitals.shape[0]
    block_count = potential.shape[0]
    piece_cells = potential.shape[1]
    width = min(plane, piece_cells)
    parts = plane // width
    capacity = CAP
    band = band_weights(side)
    entries, owners, ranks = owner_tables(frag_blocks, block_count, groups)
    count = entries.shape[1]
    slot_range = jnp.arange(capacity, dtype=jnp.int32)
    send_match = (owners[:, None, :] == me_index) & (ranks[:, None, :] == slot_range[None, :, None])
    send_block = jnp.sum(
        jnp.where(send_match, entries[:, None, :] - me_index * block_count, 0), axis=2
    ).reshape(-1)
    my_owners = lax.dynamic_index_in_dim(owners, me_index, 0, keepdims=False)
    my_ranks = lax.dynamic_index_in_dim(ranks, me_index, 0, keepdims=False)
    my_entries = lax.dynamic_index_in_dim(entries, me_index, 0, keepdims=False)
    my_slot = my_owners * capacity + my_ranks
    all_entries = entries.reshape(-1)
    weights = jnp.repeat(frag_signs, FB).astype(jnp.float32) / ORBS
    my_select = jnp.where(my_entries[:, None] == all_entries[None, :], weights[None, :], 0.0)
    block_range = jnp.arange(block_count, dtype=jnp.int32) + me_index * block_count
    owner_select = jnp.where(block_range[:, None] == all_entries[None, :], weights[None, :], 0.0)

    every = lax.all_gather(potential, "frag", axis=0, tiled=True)
    section = jnp.take(every, my_entries, axis=0)
    owned = jnp.concatenate([ion_potential, core_density], axis=1)
    outgoing = jnp.take(owned, send_block, axis=0).reshape(groups, capacity, 2 * piece_cells)
    incoming = lax.all_to_all(outgoing, "frag", split_axis=0, concat_axis=0, tiled=True)
    named = jnp.take(incoming.reshape(groups * capacity, -1), my_slot, axis=0)

    def exchange(base, core, select, gathered):
        collected = jnp.dot(
            select,
            gathered,
            precision=lax.Precision.HIGHEST,
            preferred_element_type=jnp.float32,
        )
        return base - EXCHANGE_COEF * jnp.cbrt(jnp.maximum(core + collected, DENSITY_FLOOR))

    middle = None
    filtered = None
    for iteration in range(ITERS):
        pot = lax.all_gather(section.reshape(frag_count, -1, width), "orb", axis=0)
        if parts > 1:
            pot = pot.reshape(-1, parts, frag_count, FB, width)
            pot = pot.transpose(0, 2, 3, 1, 4).reshape(-1, frag_count, FB, plane)
        pieces = []
        next_middle = []
        for frag in range(frag_count):
            if iteration == 0:
                result, dens = filter_call(True, frag, orbitals.shape, orbitals, pot, band, None)
                next_middle.append(result)
            else:
                filtered, dens = filter_call(
                    False, frag, orbitals.shape, middle[frag], pot, band, filtered
                )
            if parts > 1:
                dens = dens.reshape(-1, FB, parts, width)
                dens = dens.transpose(0, 2, 1, 3).reshape(-1, FB, width)
            if iteration == 0:
                dens = lax.all_to_all(dens, "orb", split_axis=0, concat_axis=0, tiled=True)
                dens = jnp.sum(dens, axis=0)
            pieces.append(dens)
        if iteration > 0:
            joined = jnp.concatenate(pieces, axis=1)
            joined = lax.all_to_all(joined, "orb", split_axis=0, concat_axis=0, tiled=True)
            pieces = [jnp.sum(joined, axis=0)]
        middle = next_middle
        summed = jnp.concatenate(pieces).reshape(count, piece_cells)
        gathered = lax.all_gather(summed, "frag", axis=0, tiled=True)
        if iteration + 1 < ITERS:
            section = exchange(
                named[:, :piece_cells], named[:, piece_cells:], my_select, gathered
            )
    return (filtered, exchange(ion_potential, core_density, owner_select, gathered))


def solution(mesh):
    in_specs = (
        P("frag", "orb", None, None),
        P("frag", "orb"),
        P("frag", "orb"),
        P("frag", "orb"),
        P(),
        P(),
    )
    out_specs = (P("frag", "orb", None, None), P("frag", "orb"))
    return jax.shard_map(shards, mesh=mesh, in_specs=in_specs, out_specs=out_specs, check_vma=False)
```
